32 devices in a mesh: dp: 2 (over y), expert: 16 (over z, x, core).
Axes of the slice: x: 2, y: 2, z: 4, core: 2. Of those that a mesh axis runs over, the one named last changes fastest.
Arguments:
- tokens: bfloat16 [6144, 2048], P(('dp', 'expert')), may hold values from -6 to 6
- routing: int32 [6144, 1], P(('dp', 'expert')), may hold values from 0 to 15; in each aligned block of 192 rows (0 to 191, 192 to 383, ...) at most 24 rows name the same one
- gate_scale: float32 [6144, 1], P(('dp', 'expert')), may hold values from 0.25 to 1
- cotangent: bfloat16 [6144, 2048], P(('dp', 'expert')), may hold values from -6 to 6
- up_weight: bfloat16 [16, 512, 2048], P('expert', 'dp'), may hold values from -0.125 to 0.125
- down_weight: bfloat16 [16, 512, 2048], P('expert', 'dp'), may hold values from -0.25 to 0.25
Outputs:
- output_rows: bfloat16 [6144, 2048], P(('dp', 'expert'))
- token_grad: bfloat16 [6144, 2048], P(('dp', 'expert'))
- grad_up: bfloat16 [16, 512, 2048], P('expert', 'dp')
- grad_down: bfloat16 [16, 512, 2048], P('expert', 'dp')
The draws below stay inside these ranges and needn't reach their ends.
Inputs may be any that keep to these rules, and one draw needn't show every extreme that they name: `routing`: within the 192 tokens of one device, each expert is named by at most 24 tokens, a bound that some block reaches.
All inputs are finite; a program needn't handle non-finite values.
Results may differ from the reference program's by a relative error of at most 0.014.
Values may be sent and summed in bfloat16 or wider, within the bound.
A program may use at most 64 MiB of HBM per device.

```python
import math
import jax
import jax.numpy as jnp
import numpy as np
from jax import lax

D = 2048
FF = 512
TOK_DEV = 192
EXPERTS = 16
CAP = 24
TOKENS = 6144
N_DP = 2
N_EXPERT = 16


def level_of(rng, dims, shards, low, largest):
    def one(position, parts):
        steps = jax.random.uniform(jax.random.fold_in(jax.random.fold_in(rng, 6), position), (parts,), jnp.float32, low / len(shards), largest / len(shards))
        return jnp.repeat(jnp.exp(steps), dims[position] // parts).reshape((-1,) + (1,) * (len(dims) - position - 1))

    gain = one(*shards[0])
    for cut in shards[1:]:
        gain = gain * one(*cut)
    return gain


def deal_out(own_key, own, number, rows, count, top, reach, skew):
    order = jax.random.permutation(own_key, count)
    crowded, common = load_shares(count, rows * top, reach, skew, True), load_shares(count, rows * top, reach, skew, False)
    places = jnp.arange(count)

    def named(tallies, offset_by):
        used = int((tallies > 0).sum())
        fixed = max(1, used // 4)
        moved = fixed + (places - fixed + offset_by * (used - fixed)) % max(1, count - fixed)
        return jnp.zeros((count,), jnp.int32).at[order[jnp.where(places < fixed, places, moved)]].set(jnp.asarray(tallies, jnp.int32))

    tallies = jnp.where(number % 4 == 0, named(crowded, number // 4), named(common, number - number // 4 - 1))
    mixed = jax.random.permutation(jax.random.fold_in(own, 3), count)
    giver, taker = mixed[0:count // 2 * 2:2], mixed[1:count // 2 * 2:2]
    slack = jnp.minimum(tallies[giver] - 1, reach - tallies[taker]) // 2
    slack = jnp.where((giver == order[0]) | (taker == order[0]) | (tallies[taker] == 0), 0, jnp.maximum(slack, 0))
    moved = jax.random.randint(jax.random.fold_in(own, 4), (count // 2,), 0, 1 << 20) % (slack + 1)
    tallies = tallies.at[giver].add(-moved).at[taker].add(moved)
    items = jnp.searchsorted(jnp.cumsum(tallies), jnp.arange(rows * top), side="right").astype(jnp.int32)
    listing = items.reshape(top, rows).T
    listing = listing[jax.random.permutation(jax.random.fold_in(own, 1), rows)]
    offset_by = jax.random.randint(jax.random.fold_in(own, 2), (rows, 1), 0, top)
    return jnp.take_along_axis(listing, (jnp.arange(top)[None, :] + offset_by) % top, axis=1)


def load_shares(count, total, reach, slope, full):
    portions = [(1 << 20) // math.isqrt(grade ** slope) + 1 for grade in range(1, count + 1)]
    largest = reach if full else min(reach, max(-(-total // count), total * portions[0] // sum(portions)))
    least = 1 if total - largest >= count - 1 else 0
    counts, spare = [largest] + [least] * (count - 1), total - largest - least * (count - 1)
    while spare > 0:
        free = [i for i in range(1, count) if counts[i] < largest] or [i for i in range(1, count) if counts[i] < reach]
        pool, remaining = sum([portions[i] for i in free]), spare
        for i in free:
            more = min(reach - counts[i], max(1, remaining * portions[i] // pool), spare)
            counts[i] = counts[i] + more
            spare = spare - more
    return np.array(counts)


def gaussian(own_key, dims, spread, bound, cuts=(), kind=jnp.bfloat16):
    loudness = level_of(own_key, dims, cuts, -0.22, 0.18) if cuts else 1.0
    values = jax.random.normal(own_key, dims, jnp.float32) * spread * loudness
    return jnp.minimum(jnp.maximum(values, -bound), bound).astype(kind)


def setup_inputs(seed: int = 0) -> dict:
    splits = jax.random.split(jax.random.key(seed), 7)
    tokens = gaussian(splits[0], (TOKENS, D), 1.0, 6.0, ((0, 32),))
    routing_keys = jax.random.split(jax.random.fold_in(splits[1], 1), TOKENS // TOK_DEV)
    routing_turns = jax.random.permutation(jax.random.fold_in(splits[1], 3), TOKENS // TOK_DEV)
    routing = jax.vmap(lambda own, number: deal_out(jax.random.fold_in(splits[1], 2), own, number, TOK_DEV, EXPERTS, 1, CAP, 2))(routing_keys, routing_turns).reshape((TOKENS, 1))
    gate_scale = jnp.clip(jnp.exp(math.log(1.0) - 1.3862944 * jax.random.uniform(splits[2], (TOKENS, 1), jnp.float32) ** level_of(splits[2], (TOKENS, 1), ((0, 32),), -0.2, 0.2)), 0.25, 1.0)
    cotangent = gaussian(splits[3], (TOKENS, D), 1.0, 6.0, ((0, 32),))
    up_weight = gaussian(splits[4], (EXPERTS, FF, D), D ** -0.5, 0.125, ((0, 16), (1, 2)))
    down_weight = gaussian(splits[5], (EXPERTS, FF, D), FF ** -0.5, 0.25, ((0, 16), (1, 2)))
    return {"tokens": tokens, "routing": routing, "gate_scale": gate_scale, "cotangent": cotangent, "up_weight": up_weight, "down_weight": down_weight}


def smooth(values):
    return jax.nn.gelu(values, approximate=True)

def reference(tokens, routing, gate_scale, cotangent, up_weight, down_weight):
    devices = N_DP * N_EXPERT
    ids = routing.reshape(devices, TOK_DEV).astype(jnp.int32)
    onehot = (ids[:, :, None] == jnp.arange(EXPERTS, dtype=jnp.int32)[None, None, :]).astype(jnp.int32)
    slot_rank = lax.optimization_barrier(jnp.sum(jnp.cumsum(onehot, axis=1) * onehot, axis=2)).astype(jnp.int32) - 1
    source = (jnp.arange(devices, dtype=jnp.int32) % N_EXPERT).astype(jnp.int32)
    slot_row = (source[:, None] * CAP + slot_rank).astype(jnp.int32).reshape(N_DP, N_EXPERT * TOK_DEV)
    group_ids = ids.reshape(N_DP, N_EXPERT * TOK_DEV)
    group_tokens = tokens.reshape(N_DP, N_EXPERT * TOK_DEV, D)
    scaled = (gate_scale * cotangent.astype(jnp.float32)).astype(jnp.bfloat16)
    group_scaled = scaled.reshape(N_DP, N_EXPERT * TOK_DEV, D)
    up_full = up_weight.astype(jnp.float32)
    down_full = down_weight.astype(jnp.float32)

    def group(carry, inputs):
        expert_ids, rows, inputs_tok, inputs_cot = inputs
        empty = jnp.zeros((EXPERTS, N_EXPERT * CAP, D), jnp.bfloat16)
        buffer = empty.at[expert_ids, rows].set(inputs_tok)
        dbuffer = empty.at[expert_ids, rows].set(inputs_cot)
        buffer_f = buffer.astype(jnp.float32)
        dbuffer_f = dbuffer.astype(jnp.float32)
        preact = jnp.einsum('erd,efd->erf', buffer_f, up_full)
        hidden = smooth(preact).astype(jnp.bfloat16)
        expert_out = jnp.einsum('erf,efd->erd', hidden.astype(jnp.float32), down_full).astype(jnp.bfloat16)
        hidden_grad = jnp.einsum('erd,efd->erf', dbuffer_f, down_full)
        unused, backward = jax.vjp(smooth, preact)
        preact_grad = backward(hidden_grad)[0].astype(jnp.bfloat16)
        slot_grad = jnp.einsum('erf,efd->erd', preact_grad.astype(jnp.float32), up_full).astype(jnp.bfloat16)
        term_up = jnp.einsum('erf,erd->efd', preact_grad.astype(jnp.float32), buffer_f).astype(jnp.bfloat16)
        term_down = jnp.einsum('erf,erd->efd', hidden.astype(jnp.float32), dbuffer_f).astype(jnp.bfloat16)
        new_carry = (carry[0] + term_up.astype(jnp.float32), carry[1] + term_down.astype(jnp.float32))
        return (new_carry, (expert_out[expert_ids, rows], slot_grad[expert_ids, rows]))
    start = (jnp.zeros((EXPERTS, FF, D), jnp.float32), jnp.zeros((EXPERTS, FF, D), jnp.float32))
    sums, picked = lax.scan(group, start, (group_ids, slot_row, group_tokens, group_scaled))
    out_pick = picked[0].reshape(TOKENS, D)
    grad_pick = picked[1].reshape(TOKENS, D)
    output_rows = (gate_scale * out_pick.astype(jnp.float32)).astype(jnp.bfloat16)
    return (output_rows, grad_pick, sums[0].astype(jnp.bfloat16), sums[1].astype(jnp.bfloat16))
```

```python
import functools

import jax
import jax.numpy as jnp
from jax import lax
from jax.experimental import pallas as pl
from jax.experimental.pallas import tpu as pltpu
from jax.sharding import PartitionSpec as P

MESH = pl.DeviceIdType.MESH
GROUPS = 4
UP, DOWN, TERM_DOWN, TERM_UP = range(4)
TOK, COT, OUT, GRAD = range(4)


def smooth(values):
    return jax.nn.gelu(values, approximate=True)


def dot_nt(left, right):
    return lax.dot_general(
        left, right, (((1,), (1,)), ((), ())), preferred_element_type=jnp.float32
    )


def dot_nn(left, right):
    return jnp.dot(left, right, preferred_element_type=jnp.float32)


def expert_kernel(
    n_dp, n, tok_ref, cot_ref, up_ref, down_ref,
    ret_out, ret_grad, gup_ref, gdown_ref,
    arr_tok, arr_cot, x_all, c_all, up_all, down_all, preact_all, hid_all, pg_all,
    left_t, out_buf, grad_buf, terms, landed, send_sem, recv_sem, dsend_sem, drecv_sem, local_sem,
):
    me = lax.axis_index("expert")
    mydp = lax.axis_index("dp")
    cap, width = tok_ref.shape[1], tok_ref.shape[2]
    ff = hid_all.shape[1]
    share = ff // n_dp
    slots = n // GROUPS
    rows = slots * cap

    def offset(i):
        return n // 2 + (i // 2) * (2 * (i % 2) - 1)

    def target(i):
        return lax.rem(me + offset(i), n)

    def origin(i):
        return lax.rem(me - offset(i) + n, n)

    def dispatch(stream, src, dst, i):
        peer = target(i)
        return pltpu.make_async_remote_copy(
            src_ref=src.at[peer], dst_ref=dst.at[i],
            send_sem=send_sem.at[stream, i], recv_sem=recv_sem.at[stream, i],
            device_id=(mydp, peer), device_id_type=MESH,
        )

    def give_back(stream, src, dst, i):
        peer = origin(i)
        return pltpu.make_async_remote_copy(
            src_ref=src.at[i], dst_ref=dst.at[me],
            send_sem=send_sem.at[stream, i], recv_sem=recv_sem.at[stream, i],
            device_id=(mydp, peer), device_id_type=MESH,
        )

    def dp_peer(j):
        return lax.rem(mydp + j, n_dp)

    def gather(which, src, dst, j):
        return pltpu.make_async_remote_copy(
            src_ref=src.at[0], dst_ref=dst.at[mydp],
            send_sem=dsend_sem.at[which, j], recv_sem=drecv_sem.at[which, j],
            device_id=(dp_peer(j), me), device_id_type=MESH,
        )

    def swap(which, j):
        return pltpu.make_async_remote_copy(
            src_ref=terms.at[which - TERM_DOWN, dp_peer(j)],
            dst_ref=landed.at[which - TERM_DOWN, j - 1],
            send_sem=dsend_sem.at[which, j], recv_sem=drecv_sem.at[which, j],
            device_id=(dp_peer(j), me), device_id_type=MESH,
        )

    def each(low, high, body):
        lax.fori_loop(low, high, lambda i, c: (body(i), c)[1], 0)

    own = [
        pltpu.make_async_copy(tok_ref.at[me], arr_tok.at[0], local_sem.at[0]),
        pltpu.make_async_copy(cot_ref.at[me], arr_cot.at[0], local_sem.at[1]),
        pltpu.make_async_copy(up_ref.at[0], up_all.at[mydp], local_sem.at[2]),
        pltpu.make_async_copy(down_ref.at[0], down_all.at[mydp], local_sem.at[3]),
    ]
    for copy in own:
        copy.start()

    barrier = pltpu.get_barrier_semaphore()
    each(1, n, lambda i: pl.semaphore_signal(
        barrier, inc=1, device_id=(mydp, target(i)), device_id_type=MESH))
    each(1, n_dp, lambda j: pl.semaphore_signal(
        barrier, inc=1, device_id=(dp_peer(j), me), device_id_type=MESH))
    pl.semaphore_wait(barrier, n - 1 + n_dp - 1)

    each(1, n_dp, lambda j: gather(UP, up_ref, up_all, j).start())
    each(1, n, lambda i: dispatch(TOK, tok_ref, arr_tok, i).start())
    each(1, n_dp, lambda j: gather(DOWN, down_ref, down_all, j).start())
    each(1, n, lambda i: dispatch(COT, cot_ref, arr_cot, i).start())

    for copy in own:
        copy.wait()
    each(1, n_dp, lambda j: gather(UP, up_ref, up_all, j).wait_recv())

    def take(arrived, g):
        block = arrived[pl.ds(g * slots, slots)].astype(jnp.float32)
        return block.reshape(rows, width).astype(jnp.bfloat16)

    def put(buffer, g, values):
        buffer[pl.ds(g * slots, slots)] = values.reshape(slots, cap, width).astype(jnp.bfloat16)

    def span(g):
        return pl.ds(pl.multiple_of(g * rows, rows), rows)

    def first(g):
        return jnp.where(g == 0, 1, g * slots)

    def forward(g):
        each(first(g), (g + 1) * slots, lambda i: dispatch(TOK, tok_ref, arr_tok, i).wait_recv())
        x = take(arr_tok, g)
        x_all[span(g)] = x
        preact = dot_nt(x, up_all[...].reshape(ff, width))
        preact_all[span(g)] = preact
        hidden = smooth(preact).astype(jnp.bfloat16)
        hid_all[span(g)] = hidden

    def forward_out(g):
        put(out_buf, g, dot_nn(hid_all[span(g)], down_all[...].reshape(ff, width)))
        each(first(g), (g + 1) * slots, lambda i: give_back(OUT, out_buf, ret_out, i).start())

    def backward(g):
        each(first(g), (g + 1) * slots, lambda i: dispatch(COT, cot_ref, arr_cot, i).wait_recv())
        c = take(arr_cot, g)
        c_all[span(g)] = c
        hidden_grad = dot_nt(c, down_all[...].reshape(ff, width))
        unused, pull = jax.vjp(smooth, preact_all[span(g)])
        preact_grad = pull(hidden_grad)[0].astype(jnp.bfloat16)
        pg_all[span(g)] = preact_grad
        put(grad_buf, g, dot_nn(preact_grad, up_all[...].reshape(ff, width)))
        each(first(g), (g + 1) * slots, lambda i: give_back(GRAD, grad_buf, ret_grad, i).start())

    each(0, GROUPS, forward)
    each(1, n_dp, lambda j: gather(DOWN, down_ref, down_all, j).wait_recv())
    each(0, GROUPS, forward_out)
    own_out = pltpu.make_async_copy(out_buf.at[0], ret_out.at[me], local_sem.at[0])
    own_out.start()
    each(0, GROUPS, backward)
    own_grad = pltpu.make_async_copy(grad_buf.at[0], ret_grad.at[me], local_sem.at[1])
    own_grad.start()

    def weight_terms(which, left, right):
        left_t[...] = left[...].astype(jnp.float32).T.astype(jnp.bfloat16)

        def one(j):
            q = dp_peer(j)
            block = left_t[pl.ds(pl.multiple_of(q * share, share), share)]
            terms[which - TERM_DOWN, q] = dot_nn(block, right[...]).astype(jnp.bfloat16)

        def send(j):
            one(j)
            swap(which, j).start()

        each(1, n_dp, send)
        one(0)

    def total(which, dest):
        each(1, n_dp, lambda j: swap(which, j).wait_recv())
        result = terms[which - TERM_DOWN, mydp].astype(jnp.float32)
        for j in range(1, n_dp):
            result = result + landed[which - TERM_DOWN, j - 1].astype(jnp.float32)
        dest[0] = result.astype(jnp.bfloat16)

    weight_terms(TERM_DOWN, hid_all, c_all)
    weight_terms(TERM_UP, pg_all, x_all)
    total(TERM_DOWN, gdown_ref)
    total(TERM_UP, gup_ref)

    own_out.wait()
    own_grad.wait()
    each(1, n, lambda i: give_back(OUT, out_buf, ret_out, i).wait_recv())
    each(1, n, lambda i: give_back(GRAD, grad_buf, ret_grad, i).wait_recv())

    def sent(i):
        dispatch(TOK, tok_ref, arr_tok, i).wait_send()
        dispatch(COT, cot_ref, arr_cot, i).wait_send()
        give_back(OUT, out_buf, ret_out, i).wait_send()
        give_back(GRAD, grad_buf, ret_grad, i).wait_send()

    each(1, n, sent)

    def dp_sent(j):
        gather(UP, up_ref, up_all, j).wait_send()
        gather(DOWN, down_ref, down_all, j).wait_send()
        swap(TERM_DOWN, j).wait_send()
        swap(TERM_UP, j).wait_send()

    each(1, n_dp, dp_sent)


def expert_call(tok, cot, up, down):
    n_dp, n = lax.axis_size("dp"), lax.axis_size("expert")
    cap, width = tok.shape[1], tok.shape[2]
    share = up.shape[1]
    ff, slot_total = share * n_dp, n * cap
    slab = jax.ShapeDtypeStruct((n, cap, width), jnp.bfloat16)
    weight = jax.ShapeDtypeStruct((1, share, width), jnp.bfloat16)
    hbm, vmem = pl.BlockSpec(memory_space=pl.ANY), pl.BlockSpec(memory_space=pltpu.VMEM)

    def half(*dims):
        return pltpu.VMEM(dims, jnp.bfloat16)

    return pl.pallas_call(
        functools.partial(expert_kernel, n_dp, n),
        out_shape=(slab, slab, weight, weight),
        in_specs=[hbm] * 4,
        out_specs=(hbm, hbm, vmem, vmem),
        scratch_shapes=[
            half(n, cap, width), half(n, cap, width),
            half(slot_total, width), half(slot_total, width),
            half(n_dp, share, width), half(n_dp, share, width),
            pltpu.VMEM((slot_total, ff), jnp.float32),
            half(slot_total, ff), half(slot_total, ff),
            half(ff, slot_total),
            half(n, cap, width), half(n, cap, width),
            half(2, n_dp, share, width), half(2, n_dp - 1, share, width),
            pltpu.SemaphoreType.DMA((4, n)), pltpu.SemaphoreType.DMA((4, n)),
            pltpu.SemaphoreType.DMA((4, n_dp)), pltpu.SemaphoreType.DMA((4, n_dp)),
            pltpu.SemaphoreType.DMA((4,)),
        ],
        compiler_params=pltpu.CompilerParams(
            collective_id=0, has_side_effects=True, vmem_limit_bytes=48 * 1024 * 1024
        ),
        cost_estimate=pl.CostEstimate(
            flops=12 * slot_total * width * ff, bytes_accessed=8 * slot_total * width,
            transcendentals=2 * slot_total * ff,
        ),
    )(tok, cot, up, down)


def contract_rows(left, right):
    return lax.dot_general(
        left, right, (((0,), (0,)), ((), ())), preferred_element_type=jnp.float32
    )


def per_device(tokens, routing, gate_scale, cotangent, up_weight, down_weight):
    tok_count, width = tokens.shape
    n_expert = lax.axis_size("expert")
    capacity = 2 * tok_count // n_expert
    capacity = -(-capacity // 8) * 8
    slot_total = n_expert * capacity
    ids = routing[:, 0]
    onehot = (ids[:, None] == jnp.arange(n_expert, dtype=jnp.int32)[None, :]).astype(jnp.float32)
    position = jnp.arange(tok_count, dtype=jnp.int32)
    lower_tri = (position[:, None] >= position[None, :]).astype(jnp.float32)
    counts = jnp.dot(
        lower_tri, onehot, precision=lax.Precision.HIGHEST, preferred_element_type=jnp.float32
    )
    slot_rank = (jnp.sum(counts * onehot, axis=1) - 1.0).astype(jnp.int32)
    slot_index = ids * capacity + slot_rank
    placer = (jnp.arange(slot_total, dtype=jnp.int32)[:, None] == slot_index[None, :]).astype(
        jnp.bfloat16
    )

    def place(values):
        placed = jnp.dot(placer, values, preferred_element_type=jnp.float32).astype(jnp.bfloat16)
        return placed.reshape(n_expert, capacity, width)

    scaled = (gate_scale * cotangent.astype(jnp.float32)).astype(jnp.bfloat16)
    returned, grad_back, grad_up, grad_down = expert_call(
        place(tokens), place(scaled), up_weight, down_weight
    )
    picked = contract_rows(placer, returned.reshape(slot_total, width))
    output_rows = (gate_scale * picked).astype(jnp.bfloat16)
    token_grad = contract_rows(placer, grad_back.reshape(slot_total, width)).astype(jnp.bfloat16)
    return (output_rows, token_grad, grad_up, grad_down)


def solution(mesh):
    tokens, experts = P(("dp", "expert"), None), P("expert", "dp", None)
    return jax.shard_map(
        per_device,
        mesh=mesh,
        in_specs=(tokens, tokens, tokens, tokens, experts, experts),
        out_specs=(tokens, tokens, experts, experts),
        check_vma=False,
    )
```

```python
import functools

import jax
import jax.numpy as jnp
from jax import lax
from jax.experimental import pallas as pl
from jax.experimental.pallas import tpu as pltpu
from jax.sharding import PartitionSpec as P

MESH = pl.DeviceIdType.MESH
GROUPS = 4
PLACE_BLOCKS = 4
UP, DOWN, TERM_DOWN, TERM_UP = range(4)
TOK, COT, OUT, GRAD = range(4)


def smooth(values):
    return jax.nn.gelu(values, approximate=True)


def dot_nt(left, right):
    return lax.dot_general(
        left, right, (((1,), (1,)), ((), ())), preferred_element_type=jnp.float32
    )


def dot_nn(left, right):
    return jnp.dot(left, right, preferred_element_type=jnp.float32)


def expert_kernel(
    n_dp, n, cap, ids_ref, gate_ref, tokens_hbm, cotangent_hbm, up_ref, down_ref,
    ret_out, ret_grad, gup_ref, gdown_ref, index_ref,
    tokens_ref, cotangent_ref, tok_ref, cot_ref, arr_tok, arr_cot, x_all, c_all, up_all, down_all, preact_all, hid_all, pg_all,
    placer_ref, left_t, out_buf, grad_buf, terms, landed, send_sem, recv_sem, dsend_sem, drecv_sem, local_sem,
):
    me = lax.axis_index("expert")
    mydp = lax.axis_index("dp")
    count, width = tokens_ref.shape
    ff = hid_all.shape[1]
    share = ff // n_dp
    slots = n // GROUPS
    rows = slots * cap

    def offset(i):
        return n // 2 + (i // 2) * (2 * (i % 2) - 1)

    def target(i):
        return lax.rem(me + offset(i), n)

    def origin(i):
        return lax.rem(me - offset(i) + n, n)

    def dispatch(stream, src, dst, i):
        peer = target(i)
        return pltpu.make_async_remote_copy(
            src_ref=src.at[peer], dst_ref=dst.at[i],
            send_sem=send_sem.at[stream, i], recv_sem=recv_sem.at[stream, i],
            device_id=(mydp, peer), device_id_type=MESH,
        )

    def give_back(stream, src, dst, i):
        peer = origin(i)
        return pltpu.make_async_remote_copy(
            src_ref=src.at[i], dst_ref=dst.at[me],
            send_sem=send_sem.at[stream, i], recv_sem=recv_sem.at[stream, i],
            device_id=(mydp, peer), device_id_type=MESH,
        )

    def dp_peer(j):
        return lax.rem(mydp + j, n_dp)

    def gather(which, src, dst, j):
        return pltpu.make_async_remote_copy(
            src_ref=src.at[0], dst_ref=dst.at[mydp],
            send_sem=dsend_sem.at[which, j], recv_sem=drecv_sem.at[which, j],
            device_id=(dp_peer(j), me), device_id_type=MESH,
        )

    def swap(which, j):
        return pltpu.make_async_remote_copy(
            src_ref=terms.at[which - TERM_DOWN, dp_peer(j)],
            dst_ref=landed.at[which - TERM_DOWN, j - 1],
            send_sem=dsend_sem.at[which, j], recv_sem=drecv_sem.at[which, j],
            device_id=(dp_peer(j), me), device_id_type=MESH,
        )

    def each(low, high, body):
        lax.fori_loop(low, high, lambda i, c: (body(i), c)[1], 0)

    own_tok = pltpu.make_async_copy(tok_ref.at[me], arr_tok.at[0], local_sem.at[0])
    own_cot = pltpu.make_async_copy(cot_ref.at[me], arr_cot.at[0], local_sem.at[1])
    own = [
        pltpu.make_async_copy(up_ref.at[0], up_all.at[mydp], local_sem.at[2]),
        pltpu.make_async_copy(down_ref.at[0], down_all.at[mydp], local_sem.at[3]),
    ]
    load_tok = pltpu.make_async_copy(tokens_hbm, tokens_ref, local_sem.at[4])
    load_cot = pltpu.make_async_copy(cotangent_hbm, cotangent_ref, local_sem.at[5])
    for copy in [load_tok, load_cot] + own:
        copy.start()

    barrier = pltpu.get_barrier_semaphore()
    each(1, n, lambda i: pl.semaphore_signal(
        barrier, inc=1, device_id=(mydp, target(i)), device_id_type=MESH))
    each(1, n_dp, lambda j: pl.semaphore_signal(
        barrier, inc=1, device_id=(dp_peer(j), me), device_id_type=MESH))

    ids = ids_ref[...]
    onehot = ids == lax.broadcasted_iota(jnp.int32, (n, count), 0)
    earlier = lax.broadcasted_iota(jnp.int32, (count, count), 0) < lax.broadcasted_iota(
        jnp.int32, (count, count), 1
    )
    ranks = dot_nn(
        onehot.astype(jnp.float32).astype(jnp.bfloat16),
        earlier.astype(jnp.float32).astype(jnp.bfloat16),
    )
    rank = jnp.sum(jnp.where(onehot, ranks, 0.0), axis=0, keepdims=True)
    index = ids * cap + rank.astype(jnp.int32)
    index_ref[...] = index
    placer_ref[...] = (
        (lax.broadcasted_iota(jnp.int32, (n * cap, count), 0) == index)
        .astype(jnp.float32)
        .astype(jnp.bfloat16)
    )
    block = width // PLACE_BLOCKS

    def place_tok(b):
        columns = pl.ds(pl.multiple_of(b * block, block), block)
        placed = dot_nn(placer_ref[...], tokens_ref[:, columns])
        tok_ref[:, :, columns] = placed.reshape(n, cap, block).astype(jnp.bfloat16)

    def place_cot(b):
        columns = pl.ds(pl.multiple_of(b * block, block), block)
        scaled = gate_ref[...] * cotangent_ref[:, columns].astype(jnp.float32)
        placed = dot_nn(placer_ref[...], scaled.astype(jnp.bfloat16))
        cot_ref[:, :, columns] = placed.reshape(n, cap, block).astype(jnp.bfloat16)

    load_tok.wait()
    each(0, PLACE_BLOCKS, place_tok)
    own_tok.start()
    pl.semaphore_wait(barrier, n - 1 + n_dp - 1)

    each(1, n, lambda i: dispatch(TOK, tok_ref, arr_tok, i).start())
    each(1, n_dp, lambda j: gather(UP, up_ref, up_all, j).start())
    each(1, n_dp, lambda j: gather(DOWN, down_ref, down_all, j).start())
    load_cot.wait()
    each(0, PLACE_BLOCKS, place_cot)
    own_cot.start()

    own_tok.wait()
    for copy in own:
        copy.wait()
    each(1, n_dp, lambda j: gather(UP, up_ref, up_all, j).wait_recv())

    def take(arrived, g):
        block = arrived[pl.ds(g * slots, slots)].astype(jnp.float32)
        return block.reshape(rows, width).astype(jnp.bfloat16)

    def put(buffer, g, values):
        buffer[pl.ds(g * slots, slots)] = values.reshape(slots, cap, width).astype(jnp.bfloat16)

    def span(g):
        return pl.ds(pl.multiple_of(g * rows, rows), rows)

    def first(g):
        return jnp.where(g == 0, 1, g * slots)

    def forward(g):
        low, high = first(g), (g + 1) * slots
        each(low, high, lambda i: dispatch(TOK, tok_ref, arr_tok, i).wait_recv())
        each(low, high, lambda i: dispatch(COT, cot_ref, arr_cot, i).start())
        x = take(arr_tok, g)
        x_all[span(g)] = x
        preact = dot_nt(x, up_all[...].reshape(ff, width))
        preact_all[span(g)] = preact
        hid_all[span(g)] = smooth(preact).astype(jnp.bfloat16)

    def backward(g):
        low, high = first(g), (g + 1) * slots
        put(out_buf, g, dot_nn(hid_all[span(g)], down_all[...].reshape(ff, width)))
        each(low, high, lambda i: dispatch(COT, cot_ref, arr_cot, i).wait_recv())
        each(low, high, lambda i: give_back(OUT, out_buf, ret_out, i).start())
        c = take(arr_cot, g)
        c_all[span(g)] = c
        hidden_grad = dot_nt(c, down_all[...].reshape(ff, width))
        unused, pull = jax.vjp(smooth, preact_all[span(g)])
        preact_grad = pull(hidden_grad)[0].astype(jnp.bfloat16)
        pg_all[span(g)] = preact_grad
        put(grad_buf, g, dot_nn(preact_grad, up_all[...].reshape(ff, width)))
        each(low, high, lambda i: give_back(GRAD, grad_buf, ret_grad, i).start())

    each(0, GROUPS, forward)
    own_cot.wait()
    each(1, n_dp, lambda j: gather(DOWN, down_ref, down_all, j).wait_recv())
    each(0, GROUPS, backward)
    own_out = pltpu.make_async_copy(out_buf.at[0], ret_out.at[me], local_sem.at[0])
    own_out.start()
    own_grad = pltpu.make_async_copy(grad_buf.at[0], ret_grad.at[me], local_sem.at[1])
    own_grad.start()

    def weight_terms(which, left, right):
        left_t[...] = left[...].astype(jnp.float32).T.astype(jnp.bfloat16)

        def one(j):
            q = dp_peer(j)
            block = left_t[pl.ds(pl.multiple_of(q * share, share), share)]
            terms[which - TERM_DOWN, q] = dot_nn(block, right[...]).astype(jnp.bfloat16)

        def send(j):
            one(j)
            swap(which, j).start()

        each(1, n_dp, send)
        one(0)

    def total(which, dest):
        each(1, n_dp, lambda j: swap(which, j).wait_recv())
        result = terms[which - TERM_DOWN, mydp].astype(jnp.float32)
        for j in range(1, n_dp):
            result = result + landed[which - TERM_DOWN, j - 1].astype(jnp.float32)
        dest[0] = result.astype(jnp.bfloat16)

    weight_terms(TERM_DOWN, hid_all, c_all)
    weight_terms(TERM_UP, pg_all, x_all)
    total(TERM_DOWN, gdown_ref)
    total(TERM_UP, gup_ref)

    own_out.wait()
    own_grad.wait()
    each(1, n, lambda i: give_back(OUT, out_buf, ret_out, i).wait_recv())
    each(1, n, lambda i: give_back(GRAD, grad_buf, ret_grad, i).wait_recv())

    def sent(i):
        dispatch(TOK, tok_ref, arr_tok, i).wait_send()
        dispatch(COT, cot_ref, arr_cot, i).wait_send()
        give_back(OUT, out_buf, ret_out, i).wait_send()
        give_back(GRAD, grad_buf, ret_grad, i).wait_send()

    each(1, n, sent)

    def dp_sent(j):
        gather(UP, up_ref, up_all, j).wait_send()
        gather(DOWN, down_ref, down_all, j).wait_send()
        swap(TERM_DOWN, j).wait_send()
        swap(TERM_UP, j).wait_send()

    each(1, n_dp, dp_sent)


def expert_call(cap, ids, gate, tok, cot, up, down):
    n_dp, n = lax.axis_size("dp"), lax.axis_size("expert")
    count, width = tok.shape
    share = up.shape[1]
    ff, slot_total = share * n_dp, n * cap
    slab = jax.ShapeDtypeStruct((n, cap, width), jnp.bfloat16)
    weight = jax.ShapeDtypeStruct((1, share, width), jnp.bfloat16)
    hbm, vmem = pl.BlockSpec(memory_space=pl.ANY), pl.BlockSpec(memory_space=pltpu.VMEM)

    def half(*dims):
        return pltpu.VMEM(dims, jnp.bfloat16)

    return pl.pallas_call(
        functools.partial(expert_kernel, n_dp, n, cap),
        out_shape=(slab, slab, weight, weight, jax.ShapeDtypeStruct((1, count), jnp.int32)),
        in_specs=[vmem] * 2 + [hbm] * 4,
        out_specs=(hbm, hbm, vmem, vmem, vmem),
        scratch_shapes=[
            half(count, width), half(count, width),
            half(n, cap, width), half(n, cap, width),
            half(n, cap, width), half(n, cap, width),
            half(slot_total, width), half(slot_total, width),
            half(n_dp, share, width), half(n_dp, share, width),
            pltpu.VMEM((slot_total, ff), jnp.float32),
            half(slot_total, ff), half(slot_total, ff),
            half(slot_total, count), half(ff, slot_total),
            half(n, cap, width), half(n, cap, width),
            half(2, n_dp, share, width), half(2, n_dp - 1, share, width),
            pltpu.SemaphoreType.DMA((4, n)), pltpu.SemaphoreType.DMA((4, n)),
            pltpu.SemaphoreType.DMA((4, n_dp)), pltpu.SemaphoreType.DMA((4, n_dp)),
            pltpu.SemaphoreType.DMA((6,)),
        ],
        compiler_params=pltpu.CompilerParams(
            collective_id=0, has_side_effects=True, vmem_limit_bytes=60 * 1024 * 1024
        ),
        cost_estimate=pl.CostEstimate(
            flops=12 * slot_total * width * ff, bytes_accessed=8 * slot_total * width,
            transcendentals=2 * slot_total * ff,
        ),
    )(ids, gate, tok, cot, up, down)


def contract_rows(left, right):
    return lax.dot_general(
        left, right, (((0,), (0,)), ((), ())), preferred_element_type=jnp.float32
    )


def per_device(tokens, routing, gate_scale, cotangent, up_weight, down_weight):
    tok_count, width = tokens.shape
    n_expert = lax.axis_size("expert")
    capacity = 2 * tok_count // n_expert
    capacity = -(-capacity // 8) * 8
    slot_total = n_expert * capacity
    returned, grad_back, grad_up, grad_down, slot_index = expert_call(
        capacity, routing.reshape(1, tok_count), gate_scale, tokens, cotangent, up_weight, down_weight
    )
    placer = (jnp.arange(slot_total, dtype=jnp.int32)[:, None] == slot_index).astype(jnp.bfloat16)
    picked = contract_rows(placer, returned.reshape(slot_total, width))
    output_rows = (gate_scale * picked).astype(jnp.bfloat16)
    token_grad = contract_rows(placer, grad_back.reshape(slot_total, width)).astype(jnp.bfloat16)
    return (output_rows, token_grad, grad_up, grad_down)


def solution(mesh):
    tokens, experts = P(("dp", "expert"), None), P("expert", "dp", None)
    return jax.shard_map(
        per_device,
        mesh=mesh,
        in_specs=(tokens, tokens, tokens, tokens, experts, experts),
        out_specs=(tokens, tokens, experts, experts),
        check_vma=False,
    )
```

```python
import functools

import jax
import jax.numpy as jnp
from jax import lax
from jax.experimental import pallas as pl
from jax.experimental.pallas import tpu as pltpu
from jax.sharding import PartitionSpec as P

MESH = pl.DeviceIdType.MESH
GROUPS = 4
PLACE_BLOCKS = 4
UP, DOWN, TERM_DOWN, TERM_UP = range(4)
TOK, COT, OUT, GRAD = range(4)


def smooth(values):
    return jax.nn.gelu(values, approximate=True)


def dot_nt(left, right):
    return lax.dot_general(
        left, right, (((1,), (1,)), ((), ())), preferred_element_type=jnp.float32
    )


def dot_nn(left, right):
    return jnp.dot(left, right, preferred_element_type=jnp.float32)


def expert_kernel(
    n_dp, n, cap, ids_ref, gate_ref, tokens_hbm, cotangent_hbm, up_ref, down_ref,
    rows_ref, tgrad_ref, gup_ref, gdown_ref,
    ret_out, ret_grad, placer_t, tokens_ref, cotangent_ref, tok_ref, cot_ref, arr_tok, arr_cot, x_all, c_all, up_all, down_all, preact_all, hid_all, pg_all,
    placer_ref, left_t, out_buf, grad_buf, terms, landed, send_sem, recv_sem, dsend_sem, drecv_sem, local_sem,
):
    me = lax.axis_index("expert")
    mydp = lax.axis_index("dp")
    count, width = tokens_ref.shape
    ff = hid_all.shape[1]
    share = ff // n_dp
    slots = n // GROUPS
    rows = slots * cap

    def offset(i):
        return n // 2 + (i // 2) * (2 * (i % 2) - 1)

    def target(i):
        return lax.rem(me + offset(i), n)

    def origin(i):
        return lax.rem(me - offset(i) + n, n)

    def dispatch(stream, src, dst, i):
        peer = target(i)
        return pltpu.make_async_remote_copy(
            src_ref=src.at[peer], dst_ref=dst.at[i],
            send_sem=send_sem.at[stream, i], recv_sem=recv_sem.at[stream, i],
            device_id=(mydp, peer), device_id_type=MESH,
        )

    def give_back(stream, src, dst, i):
        peer = origin(i)
        return pltpu.make_async_remote_copy(
            src_ref=src.at[i], dst_ref=dst.at[me],
            send_sem=send_sem.at[stream, i], recv_sem=recv_sem.at[stream, i],
            device_id=(mydp, peer), device_id_type=MESH,
        )

    def dp_peer(j):
        return lax.rem(mydp + j, n_dp)

    def gather(which, src, dst, j):
        return pltpu.make_async_remote_copy(
            src_ref=src.at[0], dst_ref=dst.at[mydp],
            send_sem=dsend_sem.at[which, j], recv_sem=drecv_sem.at[which, j],
            device_id=(dp_peer(j), me), device_id_type=MESH,
        )

    def swap(which, j):
        return pltpu.make_async_remote_copy(
            src_ref=terms.at[which - TERM_DOWN, dp_peer(j)],
            dst_ref=landed.at[which - TERM_DOWN, j - 1],
            send_sem=dsend_sem.at[which, j], recv_sem=drecv_sem.at[which, j],
            device_id=(dp_peer(j), me), device_id_type=MESH,
        )

    def each(low, high, body):
        lax.fori_loop(low, high, lambda i, c: (body(i), c)[1], 0)

    own_tok = pltpu.make_async_copy(tok_ref.at[me], arr_tok.at[0], local_sem.at[0])
    own_cot = pltpu.make_async_copy(cot_ref.at[me], arr_cot.at[0], local_sem.at[1])
    own = [
        pltpu.make_async_copy(up_ref.at[0], up_all.at[mydp], local_sem.at[2]),
        pltpu.make_async_copy(down_ref.at[0], down_all.at[mydp], local_sem.at[3]),
    ]
    load_tok = pltpu.make_async_copy(tokens_hbm, tokens_ref, local_sem.at[4])
    load_cot = pltpu.make_async_copy(cotangent_hbm, cotangent_ref, local_sem.at[5])
    for copy in [load_tok, load_cot] + own:
        copy.start()

    barrier = pltpu.get_barrier_semaphore()
    each(1, n, lambda i: pl.semaphore_signal(
        barrier, inc=1, device_id=(mydp, target(i)), device_id_type=MESH))
    each(1, n_dp, lambda j: pl.semaphore_signal(
        barrier, inc=1, device_id=(dp_peer(j), me), device_id_type=MESH))

    ids = ids_ref[...]
    onehot = ids == lax.broadcasted_iota(jnp.int32, (n, count), 0)
    earlier = lax.broadcasted_iota(jnp.int32, (count, count), 0) < lax.broadcasted_iota(
        jnp.int32, (count, count), 1
    )
    ranks = dot_nn(
        onehot.astype(jnp.float32).astype(jnp.bfloat16),
        earlier.astype(jnp.float32).astype(jnp.bfloat16),
    )
    rank = jnp.sum(jnp.where(onehot, ranks, 0.0), axis=0, keepdims=True)
    index = ids * cap + rank.astype(jnp.int32)
    placer_ref[...] = (
        (lax.broadcasted_iota(jnp.int32, (n * cap, count), 0) == index)
        .astype(jnp.float32)
        .astype(jnp.bfloat16)
    )
    block = width // PLACE_BLOCKS

    def gate_column():
        return jnp.broadcast_to(gate_ref[...], (8, count)).T[:, :1]

    def place_tok(b):
        columns = pl.ds(pl.multiple_of(b * block, block), block)
        placed = dot_nn(placer_ref[...], tokens_ref[:, columns])
        tok_ref[:, :, columns] = placed.reshape(n, cap, block).astype(jnp.bfloat16)

    def place_cot(b):
        columns = pl.ds(pl.multiple_of(b * block, block), block)
        scaled = gate_column() * cotangent_ref[:, columns].astype(jnp.float32)
        placed = dot_nn(placer_ref[...], scaled.astype(jnp.bfloat16))
        cot_ref[:, :, columns] = placed.reshape(n, cap, block).astype(jnp.bfloat16)

    load_tok.wait()
    each(0, PLACE_BLOCKS, place_tok)
    own_tok.start()
    pl.semaphore_wait(barrier, n - 1 + n_dp - 1)

    each(1, n, lambda i: dispatch(TOK, tok_ref, arr_tok, i).start())
    each(1, n_dp, lambda j: gather(UP, up_ref, up_all, j).start())
    each(1, n_dp, lambda j: gather(DOWN, down_ref, down_all, j).start())
    load_cot.wait()
    each(0, PLACE_BLOCKS, place_cot)
    own_cot.start()
    placer_t[...] = placer_ref[...].astype(jnp.float32).T.astype(jnp.bfloat16)

    def pick(b, returned):
        columns = pl.ds(pl.multiple_of(b * block, block), block)
        values = returned[:, :, columns].astype(jnp.float32).reshape(n * cap, block)
        return columns, dot_nn(placer_t[...], values.astype(jnp.bfloat16))

    def pick_rows(b):
        columns, picked = pick(b, ret_out)
        rows_ref[:, columns] = (gate_column() * picked).astype(jnp.bfloat16)

    def pick_grad(b):
        columns, picked = pick(b, ret_grad)
        tgrad_ref[:, columns] = picked.astype(jnp.bfloat16)

    own_tok.wait()
    for copy in own:
        copy.wait()
    each(1, n_dp, lambda j: gather(UP, up_ref, up_all, j).wait_recv())

    def take(arrived, g):
        block = arrived[pl.ds(g * slots, slots)].astype(jnp.float32)
        return block.reshape(rows, width).astype(jnp.bfloat16)

    def put(buffer, g, values):
        buffer[pl.ds(g * slots, slots)] = values.reshape(slots, cap, width).astype(jnp.bfloat16)

    def span(g):
        return pl.ds(pl.multiple_of(g * rows, rows), rows)

    def first(g):
        return jnp.where(g == 0, 1, g * slots)

    def forward(g):
        low, high = first(g), (g + 1) * slots
        each(low, high, lambda i: dispatch(TOK, tok_ref, arr_tok, i).wait_recv())
        each(low, high, lambda i: dispatch(COT, cot_ref, arr_cot, i).start())
        x = take(arr_tok, g)
        x_all[span(g)] = x
        preact = dot_nt(x, up_all[...].reshape(ff, width))
        preact_all[span(g)] = preact
        hid_all[span(g)] = smooth(preact).astype(jnp.bfloat16)

    def backward(g):
        low, high = first(g), (g + 1) * slots
        put(out_buf, g, dot_nn(hid_all[span(g)], down_all[...].reshape(ff, width)))
        each(low, high, lambda i: dispatch(COT, cot_ref, arr_cot, i).wait_recv())
        each(low, high, lambda i: give_back(OUT, out_buf, ret_out, i).start())
        c = take(arr_cot, g)
        c_all[span(g)] = c
        hidden_grad = dot_nt(c, down_all[...].reshape(ff, width))
        unused, pull = jax.vjp(smooth, preact_all[span(g)])
        preact_grad = pull(hidden_grad)[0].astype(jnp.bfloat16)
        pg_all[span(g)] = preact_grad
        put(grad_buf, g, dot_nn(preact_grad, up_all[...].reshape(ff, width)))
        each(low, high, lambda i: give_back(GRAD, grad_buf, ret_grad, i).start())

    each(0, GROUPS, forward)
    own_cot.wait()
    each(1, n_dp, lambda j: gather(DOWN, down_ref, down_all, j).wait_recv())
    each(0, GROUPS, backward)
    own_out = pltpu.make_async_copy(out_buf.at[0], ret_out.at[me], local_sem.at[0])
    own_out.start()
    own_grad = pltpu.make_async_copy(grad_buf.at[0], ret_grad.at[me], local_sem.at[1])
    own_grad.start()

    def weight_terms(which, left, right):
        left_t[...] = left[...].astype(jnp.float32).T.astype(jnp.bfloat16)

        def one(j):
            q = dp_peer(j)
            block = left_t[pl.ds(pl.multiple_of(q * share, share), share)]
            terms[which - TERM_DOWN, q] = dot_nn(block, right[...]).astype(jnp.bfloat16)

        def send(j):
            one(j)
            swap(which, j).start()

        each(1, n_dp, send)
        one(0)

    def total(which, dest):
        each(1, n_dp, lambda j: swap(which, j).wait_recv())
        result = terms[which - TERM_DOWN, mydp].astype(jnp.float32)
        for j in range(1, n_dp):
            result = result + landed[which - TERM_DOWN, j - 1].astype(jnp.float32)
        dest[0] = result.astype(jnp.bfloat16)

    weight_terms(TERM_DOWN, hid_all, c_all)
    weight_terms(TERM_UP, pg_all, x_all)
    own_out.wait()
    own_grad.wait()
    each(1, n, lambda i: give_back(OUT, out_buf, ret_out, i).wait_recv())
    each(0, PLACE_BLOCKS, pick_rows)
    total(TERM_DOWN, gdown_ref)
    total(TERM_UP, gup_ref)
    each(1, n, lambda i: give_back(GRAD, grad_buf, ret_grad, i).wait_recv())
    each(0, PLACE_BLOCKS, pick_grad)

    def sent(i):
        dispatch(TOK, tok_ref, arr_tok, i).wait_send()
        dispatch(COT, cot_ref, arr_cot, i).wait_send()
        give_back(OUT, out_buf, ret_out, i).wait_send()
        give_back(GRAD, grad_buf, ret_grad, i).wait_send()

    each(1, n, sent)

    def dp_sent(j):
        gather(UP, up_ref, up_all, j).wait_send()
        gather(DOWN, down_ref, down_all, j).wait_send()
        swap(TERM_DOWN, j).wait_send()
        swap(TERM_UP, j).wait_send()

    each(1, n_dp, dp_sent)


def expert_call(cap, ids, gate, tok, cot, up, down):
    n_dp, n = lax.axis_size("dp"), lax.axis_size("expert")
    count, width = tok.shape
    share = up.shape[1]
    ff, slot_total = share * n_dp, n * cap
    result = jax.ShapeDtypeStruct((count, width), jnp.bfloat16)
    weight = jax.ShapeDtypeStruct((1, share, width), jnp.bfloat16)
    hbm, vmem = pl.BlockSpec(memory_space=pl.ANY), pl.BlockSpec(memory_space=pltpu.VMEM)

    def half(*dims):
        return pltpu.VMEM(dims, jnp.bfloat16)

    return pl.pallas_call(
        functools.partial(expert_kernel, n_dp, n, cap),
        out_shape=(result, result, weight, weight),
        in_specs=[vmem] * 2 + [hbm] * 4,
        out_specs=(vmem, vmem, vmem, vmem),
        scratch_shapes=[
            half(n, cap, width), half(n, cap, width), half(count, slot_total),
            half(count, width), half(count, width),
            half(n, cap, width), half(n, cap, width),
            half(n, cap, width), half(n, cap, width),
            half(slot_total, width), half(slot_total, width),
            half(n_dp, share, width), half(n_dp, share, width),
            pltpu.VMEM((slot_total, ff), jnp.float32),
            half(slot_total, ff), half(slot_total, ff),
            half(slot_total, count), half(ff, slot_total),
            half(n, cap, width), half(n, cap, width),
            half(2, n_dp, share, width), half(2, n_dp - 1, share, width),
            pltpu.SemaphoreType.DMA((4, n)), pltpu.SemaphoreType.DMA((4, n)),
            pltpu.SemaphoreType.DMA((4, n_dp)), pltpu.SemaphoreType.DMA((4, n_dp)),
            pltpu.SemaphoreType.DMA((6,)),
        ],
        compiler_params=pltpu.CompilerParams(
            collective_id=0, has_side_effects=True, vmem_limit_bytes=60 * 1024 * 1024
        ),
        cost_estimate=pl.CostEstimate(
            flops=12 * slot_total * width * ff, bytes_accessed=8 * slot_total * width,
            transcendentals=2 * slot_total * ff,
        ),
    )(ids, gate, tok, cot, up, down)


def per_device(tokens, routing, gate_scale, cotangent, up_weight, down_weight):
    tok_count = tokens.shape[0]
    n_expert = lax.axis_size("expert")
    capacity = 2 * tok_count // n_expert
    capacity = -(-capacity // 8) * 8
    row = (1, tok_count)
    return expert_call(
        capacity, routing.reshape(row), gate_scale.reshape(row), tokens, cotangent,
        up_weight, down_weight,
    )


def solution(mesh):
    tokens, experts = P(("dp", "expert"), None), P("expert", "dp", None)
    return jax.shard_map(
        per_device,
        mesh=mesh,
        in_specs=(tokens, tokens, tokens, tokens, experts, experts),
        out_specs=(tokens, tokens, experts, experts),
        check_vma=False,
    )
```

```python
import functools

import jax
import jax.numpy as jnp
from jax import lax
from jax.experimental import pallas as pl
from jax.experimental.pallas import tpu as pltpu
from jax.sharding import PartitionSpec as P

MESH = pl.DeviceIdType.MESH
GROUPS = 4
PLACE_BLOCKS = 4
UP, DOWN, TERM_DOWN, TERM_UP = range(4)
TOK, COT, OUT, GRAD = range(4)


def smooth(values):
    return jax.nn.gelu(values, approximate=True)


def dot_nt(left, right):
    return lax.dot_general(
        left, right, (((1,), (1,)), ((), ())), preferred_element_type=jnp.float32
    )


def dot_nn(left, right):
    return jnp.dot(left, right, preferred_element_type=jnp.float32)


def expert_kernel(
    n_dp, n, cap, ids_ref, gate_ref, tokens_hbm, cotangent_hbm, up_ref, down_ref,
    rows_ref, tgrad_ref, gup_ref, gdown_ref,
    ret_out, ret_grad, placer_t, tokens_ref, cotangent_ref, tok_ref, cot_ref, arr_tok, arr_cot, x_all, c_all, up_all, down_all, preact_all, hid_all, pg_all,
    placer_ref, left_t, out_buf, grad_buf, terms, landed, send_sem, recv_sem, dsend_sem, drecv_sem, local_sem,
):
    me = lax.axis_index("expert")
    mydp = lax.axis_index("dp")
    count, width = tokens_ref.shape
    ff = hid_all.shape[1]
    share = ff // n_dp
    slots = n // GROUPS
    rows = slots * cap

    def offset(i):
        return n // 2 + (i // 2) * (2 * (i % 2) - 1)

    def target(i):
        return lax.rem(me + offset(i), n)

    def origin(i):
        return lax.rem(me - offset(i) + n, n)

    def dispatch(stream, src, dst, i):
        peer = target(i)
        return pltpu.make_async_remote_copy(
            src_ref=src.at[peer], dst_ref=dst.at[i],
            send_sem=send_sem.at[stream, i], recv_sem=recv_sem.at[stream, i],
            device_id=(mydp, peer), device_id_type=MESH,
        )

    def give_back(stream, src, dst, i):
        peer = origin(i)
        return pltpu.make_async_remote_copy(
            src_ref=src.at[i], dst_ref=dst.at[me],
            send_sem=send_sem.at[stream, i], recv_sem=recv_sem.at[stream, i],
            device_id=(mydp, peer), device_id_type=MESH,
        )

    def dp_peer(j):
        return lax.rem(mydp + j, n_dp)

    def gather(which, src, dst, j):
        return pltpu.make_async_remote_copy(
            src_ref=src.at[0], dst_ref=dst.at[mydp],
            send_sem=dsend_sem.at[which, j], recv_sem=drecv_sem.at[which, j],
            device_id=(dp_peer(j), me), device_id_type=MESH,
        )

    def swap(which, j):
        return pltpu.make_async_remote_copy(
            src_ref=terms.at[which - TERM_DOWN, dp_peer(j)],
            dst_ref=landed.at[which - TERM_DOWN, j - 1],
            send_sem=dsend_sem.at[which, j], recv_sem=drecv_sem.at[which, j],
            device_id=(dp_peer(j), me), device_id_type=MESH,
        )

    def each(low, high, body):
        lax.fori_loop(low, high, lambda i, c: (body(i), c)[1], 0)

    own_tok = pltpu.make_async_copy(tok_ref.at[me], arr_tok.at[0], local_sem.at[0])
    own_cot = pltpu.make_async_copy(cot_ref.at[me], arr_cot.at[0], local_sem.at[1])
    own = [
        pltpu.make_async_copy(up_ref.at[0], up_all.at[mydp], local_sem.at[2]),
        pltpu.make_async_copy(down_ref.at[0], down_all.at[mydp], local_sem.at[3]),
    ]
    load_tok = pltpu.make_async_copy(tokens_hbm, tokens_ref, local_sem.at[4])
    load_cot = pltpu.make_async_copy(cotangent_hbm, cotangent_ref, local_sem.at[5])
    for copy in [load_tok, load_cot] + own:
        copy.start()

    barrier = pltpu.get_barrier_semaphore()
    each(1, n, lambda i: pl.semaphore_signal(
        barrier, inc=1, device_id=(mydp, target(i)), device_id_type=MESH))
    each(1, n_dp, lambda j: pl.semaphore_signal(
        barrier, inc=1, device_id=(dp_peer(j), me), device_id_type=MESH))

    ids = ids_ref[...]
    onehot = ids == lax.broadcasted_iota(jnp.int32, (n, count), 0)
    earlier = lax.broadcasted_iota(jnp.int32, (count, count), 0) < lax.broadcasted_iota(
        jnp.int32, (count, count), 1
    )
    ranks = dot_nn(
        onehot.astype(jnp.float32).astype(jnp.bfloat16),
        earlier.astype(jnp.float32).astype(jnp.bfloat16),
    )
    rank = jnp.sum(jnp.where(onehot, ranks, 0.0), axis=0, keepdims=True)
    index = ids * cap + rank.astype(jnp.int32)
    placer_ref[...] = (
        (lax.broadcasted_iota(jnp.int32, (n * cap, count), 0) == index)
        .astype(jnp.float32)
        .astype(jnp.bfloat16)
    )
    block = width // PLACE_BLOCKS

    def gate_column():
        return jnp.broadcast_to(gate_ref[...], (8, count)).T[:, :1]

    def place_tok(b):
        columns = pl.ds(pl.multiple_of(b * block, block), block)
        placed = dot_nn(placer_ref[...], tokens_ref[:, columns])
        tok_ref[:, :, columns] = placed.reshape(n, cap, block).astype(jnp.bfloat16)

    def place_cot(b):
        columns = pl.ds(pl.multiple_of(b * block, block), block)
        scaled = gate_column() * cotangent_ref[:, columns].astype(jnp.float32)
        placed = dot_nn(placer_ref[...], scaled.astype(jnp.bfloat16))
        cot_ref[:, :, columns] = placed.reshape(n, cap, block).astype(jnp.bfloat16)

    load_tok.wait()
    each(0, PLACE_BLOCKS, place_tok)
    own_tok.start()
    pl.semaphore_wait(barrier, n - 1 + n_dp - 1)

    each(1, n, lambda i: dispatch(TOK, tok_ref, arr_tok, i).start())
    each(1, n_dp, lambda j: gather(UP, up_ref, up_all, j).start())
    each(1, n_dp, lambda j: gather(DOWN, down_ref, down_all, j).start())
    load_cot.wait()
    each(0, PLACE_BLOCKS, place_cot)
    own_cot.start()
    placer_t[...] = placer_ref[...].astype(jnp.float32).T.astype(jnp.bfloat16)

    def pick(b, returned):
        columns = pl.ds(pl.multiple_of(b * block, block), block)
        values = returned[:, :, columns].astype(jnp.float32).reshape(n * cap, block)
        return columns, dot_nn(placer_t[...], values.astype(jnp.bfloat16))

    def pick_rows(b):
        columns, picked = pick(b, ret_out)
        rows_ref[:, columns] = (gate_column() * picked).astype(jnp.bfloat16)

    def pick_grad(b):
        columns, picked = pick(b, ret_grad)
        tgrad_ref[:, columns] = picked.astype(jnp.bfloat16)

    own_tok.wait()
    for copy in own:
        copy.wait()
    each(1, n_dp, lambda j: gather(UP, up_ref, up_all, j).wait_recv())

    def take(arrived, g):
        block = arrived[pl.ds(g * slots, slots)].astype(jnp.float32)
        return block.reshape(rows, width).astype(jnp.bfloat16)

    def put(buffer, g, values):
        buffer[pl.ds(g * slots, slots)] = values.reshape(slots, cap, width).astype(jnp.bfloat16)

    def span(g):
        return pl.ds(pl.multiple_of(g * rows, rows), rows)

    def first(g):
        return jnp.where(g == 0, 1, g * slots)

    def forward(g):
        low, high = first(g), (g + 1) * slots
        each(low, high, lambda i: dispatch(TOK, tok_ref, arr_tok, i).wait_recv())
        each(low, high, lambda i: dispatch(COT, cot_ref, arr_cot, i).start())
        x = take(arr_tok, g)
        x_all[span(g)] = x
        preact = dot_nt(x, up_all[...].reshape(ff, width))
        preact_all[span(g)] = preact
        hid_all[span(g)] = smooth(preact).astype(jnp.bfloat16)

    def backward(g):
        low, high = first(g), (g + 1) * slots
        put(out_buf, g, dot_nn(hid_all[span(g)], down_all[...].reshape(ff, width)))
        each(low, high, lambda i: dispatch(COT, cot_ref, arr_cot, i).wait_recv())
        each(low, high, lambda i: give_back(OUT, out_buf, ret_out, i).start())
        c = take(arr_cot, g)
        c_all[span(g)] = c
        hidden_grad = dot_nt(c, down_all[...].reshape(ff, width))
        unused, pull = jax.vjp(smooth, preact_all[span(g)])
        preact_grad = pull(hidden_grad)[0].astype(jnp.bfloat16)
        pg_all[span(g)] = preact_grad
        put(grad_buf, g, dot_nn(preact_grad, up_all[...].reshape(ff, width)))
        each(low, high, lambda i: give_back(GRAD, grad_buf, ret_grad, i).start())

    each(0, GROUPS, forward)
    own_cot.wait()
    each(1, n_dp, lambda j: gather(DOWN, down_ref, down_all, j).wait_recv())
    each(0, GROUPS, backward)
    own_out = pltpu.make_async_copy(out_buf.at[0], ret_out.at[me], local_sem.at[0])
    own_out.start()
    own_grad = pltpu.make_async_copy(grad_buf.at[0], ret_grad.at[me], local_sem.at[1])
    own_grad.start()

    def weight_terms(which, left, right):
        left_t[...] = left[...].astype(jnp.float32).T.astype(jnp.bfloat16)

        def one(j):
            q = dp_peer(j)
            block = left_t[pl.ds(pl.multiple_of(q * share, share), share)]
            terms[which - TERM_DOWN, q] = dot_nn(block, right[...]).astype(jnp.bfloat16)

        def send(j):
            one(j)
            swap(which, j).start()

        each(1, n_dp, send)
        one(0)

    def total(which, dest):
        each(1, n_dp, lambda j: swap(which, j).wait_recv())
        result = terms[which - TERM_DOWN, mydp].astype(jnp.float32)
        for j in range(1, n_dp):
            result = result + landed[which - TERM_DOWN, j - 1].astype(jnp.float32)
        dest[0] = result.astype(jnp.bfloat16)

    weight_terms(TERM_DOWN, hid_all, c_all)
    weight_terms(TERM_UP, pg_all, x_all)
    own_out.wait()
    own_grad.wait()
    each(1, n, lambda i: give_back(OUT, out_buf, ret_out, i).wait_recv())
    each(0, PLACE_BLOCKS, pick_rows)
    total(TERM_DOWN, gdown_ref)
    total(TERM_UP, gup_ref)
    each(1, n, lambda i: give_back(GRAD, grad_buf, ret_grad, i).wait_recv())
    each(0, PLACE_BLOCKS, pick_grad)

    def sent(i):
        dispatch(TOK, tok_ref, arr_tok, i).wait_send()
        dispatch(COT, cot_ref, arr_cot, i).wait_send()
        give_back(OUT, out_buf, ret_out, i).wait_send()
        give_back(GRAD, grad_buf, ret_grad, i).wait_send()

    each(1, n, sent)

    def dp_sent(j):
        gather(UP, up_ref, up_all, j).wait_send()
        gather(DOWN, down_ref, down_all, j).wait_send()
        swap(TERM_DOWN, j).wait_send()
        swap(TERM_UP, j).wait_send()

    each(1, n_dp, dp_sent)


def expert_call(cap, ids, gate, tok, cot, up, down):
    n_dp, n = lax.axis_size("dp"), lax.axis_size("expert")
    count, width = tok.shape
    share = up.shape[1]
    ff, slot_total = share * n_dp, n * cap
    result = jax.ShapeDtypeStruct((count, width), jnp.bfloat16)
    weight = jax.ShapeDtypeStruct((1, share, width), jnp.bfloat16)
    hbm, vmem = pl.BlockSpec(memory_space=pl.ANY), pl.BlockSpec(memory_space=pltpu.VMEM)

    def half(*dims):
        return pltpu.VMEM(dims, jnp.bfloat16)

    return pl.pallas_call(
        functools.partial(expert_kernel, n_dp, n, cap),
        out_shape=(result, result, weight, weight),
        in_specs=[vmem] * 2 + [hbm] * 4,
        out_specs=(vmem, vmem, vmem, vmem),
        scratch_shapes=[
            half(n, cap, width), half(n, cap, width), half(count, slot_total),
            half(count, width), half(count, width),
            half(n, cap, width), half(n, cap, width),
            half(n, cap, width), half(n, cap, width),
            half(slot_total, width), half(slot_total, width),
            half(n_dp, share, width), half(n_dp, share, width),
            pltpu.VMEM((slot_total, ff), jnp.float32),
            half(slot_total, ff), half(slot_total, ff),
            half(slot_total, count), half(ff, slot_total),
            half(n, cap, width), half(n, cap, width),
            half(2, n_dp, share, width), half(2, n_dp - 1, share, width),
            pltpu.SemaphoreType.DMA((4, n)), pltpu.SemaphoreType.DMA((4, n)),
            pltpu.SemaphoreType.DMA((4, n_dp)), pltpu.SemaphoreType.DMA((4, n_dp)),
            pltpu.SemaphoreType.DMA((6,)),
        ],
        compiler_params=pltpu.CompilerParams(
            collective_id=0, has_side_effects=True, vmem_limit_bytes=48 * 1024 * 1024
        ),
        cost_estimate=pl.CostEstimate(
            flops=12 * slot_total * width * ff, bytes_accessed=8 * slot_total * width,
            transcendentals=2 * slot_total * ff,
        ),
    )(ids, gate, tok, cot, up, down)


def per_device(tokens, routing, gate_scale, cotangent, up_weight, down_weight):
    tok_count = tokens.shape[0]
    n_expert = lax.axis_size("expert")
    capacity = 2 * tok_count // n_expert
    capacity = -(-capacity // 8) * 8
    row = (1, tok_count)
    return expert_call(
        capacity, routing.reshape(row), gate_scale.reshape(row), tokens, cotangent,
        up_weight, down_weight,
    )


def solution(mesh):
    tokens, experts = P(("dp", "expert"), None), P("expert", "dp", None)
    return jax.shard_map(
        per_device,
        mesh=mesh,
        in_specs=(tokens, tokens, tokens, tokens, experts, experts),
        out_specs=(tokens, tokens, experts, experts),
        check_vma=False,
    )
```
